256 devices in a mesh: dp: 4 (over x), fsdp: 64 (over z, y, core).
Axes of the slice: x: 4, y: 4, z: 8, core: 2. Of those that a mesh axis runs over, the one named last changes fastest.
Arguments:
- grad_parts: bfloat16 [4, 144, 1024, 1024], P('dp', None, 'fsdp'), may hold values from -64 to 64
- factors: bfloat16 [4, 64, 1, 2, 1024, 1024], P('dp', 'fsdp'), may hold values from -1 to 6
- weights: bfloat16 [144, 1024, 1024], P('dp', 'fsdp'), may hold values from -0.0625 to 0.0625
- block_owner: int32 [144], replicated, may hold values from 0 to 63, as said below
Outputs:
- recast: bfloat16 [144, 1024, 1024], P('dp', 'fsdp')
The draws below stay inside these ranges and needn't reach their ends.
Inputs may be any that keep to these rules, and one draw needn't show every extreme that they name: `block_owner`: blocks of group g are g * 36 to (g + 1) * 36 - 1. Within each group no fsdp index owns more than 1 block, and in every group one owns exactly 1.
All inputs are finite; a program needn't handle non-finite values.
Results may differ from the reference program's by a relative error of at most 0.028.
Values may be sent and summed in bfloat16 or wider, within the bound.
A program may use at most 64 MiB of HBM per device.

```python
import math
import jax
import jax.numpy as jnp
from jax import lax

D = 8192
BS = 1024
QB = 64
KB = 8
BLOCKS = 144
GB = 36
SLOTS = 1
N_DP = 4
N_FSDP = 64


def draw_grad_parts(key, part):
    key = jax.random.fold_in(key, 11)
    sub_keys = jax.random.split(key, 3)
    base_noise = jax.random.truncated_normal(sub_keys[0], -4.0, 4.0, (N_DP, BLOCKS, BS, BS), jnp.float32)
    row_rand = jnp.exp(jax.random.uniform(sub_keys[1], (1, BLOCKS, BS, 1)) * math.log(10.0))
    col_rand = jnp.exp(jax.random.uniform(sub_keys[2], (1, BLOCKS, 1, BS)) * math.log(3.0))
    row_ramp = jnp.exp(0.5 * math.log(3.0) * jnp.arange(BS, dtype=jnp.float32) / BS).reshape(1, 1, BS, 1)
    block_ramp = jnp.exp(0.5 * math.log(3.0) * jnp.arange(BLOCKS, dtype=jnp.float32) / BLOCKS).reshape(1, BLOCKS, 1, 1)
    values = 0.25 * base_noise * row_rand * col_rand * row_ramp * block_ramp
    return jnp.clip(values, -64.0, 64.0).astype(jnp.bfloat16)


def draw_factors(key, part):
    key = jax.random.fold_in(key, 23)
    sub_keys = jax.random.split(key, 2)
    full_shape = (N_DP, N_FSDP, SLOTS, 2, BS, BS)
    low_end = math.log(0.3)
    high_end = math.log(3.0)
    off_diag = jax.random.truncated_normal(sub_keys[0], -4.0, 4.0, full_shape, jnp.float32)
    diagonal = jnp.exp(jax.random.uniform(sub_keys[1], (N_DP, N_FSDP, SLOTS, 2, BS), minval=low_end, maxval=high_end))
    positions = jnp.arange(BS, dtype=jnp.int32)
    identity = (positions[:, None] == positions[None, :]).astype(jnp.float32)
    values = 0.4 * off_diag / math.sqrt(BS) + diagonal[..., None] * identity
    return values.astype(jnp.bfloat16)


def owner_group(key):
    sub_keys = jax.random.split(key, 3)
    device_order = jax.random.permutation(sub_keys[0], N_FSDP).astype(jnp.int32)
    labels = jax.random.permutation(sub_keys[1], (N_FSDP - 1) * SLOTS).astype(jnp.int32)
    others = device_order[1 + labels % (N_FSDP - 1)]
    sequence = jnp.concatenate([jnp.full((SLOTS,), device_order[0], jnp.int32), others[:GB - SLOTS]])
    places = jax.random.permutation(sub_keys[2], GB).astype(jnp.int32)
    return sequence[places]


def draw_block_owner(key, part):
    key = jax.random.fold_in(key, 37)
    group_keys = jax.random.split(key, N_DP)
    return jax.vmap(owner_group)(group_keys).reshape(BLOCKS).astype(jnp.int32)


def level_of(own_key, dims, cuts, least, high):
    factor_of = 1.0
    for dim, blocks in cuts:
        heights = jax.random.uniform(jax.random.fold_in(jax.random.fold_in(own_key, 6), dim), (blocks,), jnp.float32, least / len(cuts), high / len(cuts))
        factor_of = factor_of * jnp.repeat(jnp.exp(heights), dims[dim] // blocks).reshape((-1,) + (1,) * (len(dims) - 1 - dim))
    return factor_of


def scatter_about(own_key, dims, width, bound, cuts=(), kind=jnp.bfloat16):
    values = jax.random.normal(own_key, dims, jnp.float32) * width
    if len(cuts) > 0:
        values = level_of(own_key, dims, cuts, -0.22, 0.18) * values
    return jnp.clip(values, min=-bound, max=bound).astype(kind)


def setup_inputs(seed: int = 0) -> dict:
    splits = jax.random.split(jax.random.key(seed), 5)
    grad_parts = draw_grad_parts(jax.random.fold_in(splits[4], 71), 0)
    factors = draw_factors(jax.random.fold_in(splits[4], 71), 0)
    weights = scatter_about(splits[2], (BLOCKS, BS, BS), D ** -0.5, 0.0625, ((0, 4), (1, 64)))
    block_owner = draw_block_owner(jax.random.fold_in(splits[4], 71), 0)
    return {"grad_parts": grad_parts, "factors": factors, "weights": weights, "block_owner": block_owner}


learn_rate = 0.02
small_eps = 1e-06

def reference(grad_parts, factors, weights, block_owner):
    summed_grad = lax.optimization_barrier(jnp.sum(grad_parts.astype(jnp.float32), axis=0)).astype(jnp.bfloat16)
    grad_wide = summed_grad.astype(jnp.float32)
    squares_sum = jnp.sum(grad_wide * grad_wide)
    global_scale = 0.5 * math.sqrt(float(BLOCKS * BS * BS)) / jnp.sqrt(squares_sum)
    blocks = jnp.arange(BLOCKS, dtype=jnp.int32)
    group_index = (blocks // GB).astype(jnp.int32)
    earlier_same = (block_owner[:, None] == block_owner[None, :]) & (group_index[:, None] == group_index[None, :]) & (blocks[None, :] < blocks[:, None])
    slot_of = lax.optimization_barrier(jnp.sum(earlier_same.astype(jnp.int32), axis=1)).astype(jnp.int32)

    def one_block(block_index):
        left_factor = factors[group_index[block_index], block_owner[block_index], slot_of[block_index], 0]
        right_factor = factors[group_index[block_index], block_owner[block_index], slot_of[block_index], 1]
        block_grad = summed_grad[block_index]
        right_product = jnp.dot(block_grad, right_factor, preferred_element_type=jnp.float32).astype(jnp.bfloat16)
        precond = jnp.dot(left_factor, right_product, preferred_element_type=jnp.float32)
        block_wide = block_grad.astype(jnp.float32)
        graft_ratio = jnp.sqrt((jnp.mean(block_wide * block_wide) + small_eps) / (jnp.mean(precond * precond) + small_eps))
        update = (global_scale * graft_ratio * precond).astype(jnp.bfloat16)
        return (weights[block_index].astype(jnp.float32) - learn_rate * update.astype(jnp.float32)).astype(jnp.bfloat16)
    new_weight = lax.map(one_block, blocks)
    tensor_id = (blocks >= QB).astype(jnp.int32) + (blocks >= QB + KB).astype(jnp.int32) + (blocks >= QB + 2 * KB).astype(jnp.int32)
    tensor_range = jnp.arange(4, dtype=jnp.int32)
    block_peak = lax.optimization_barrier(jnp.max(jnp.abs(new_weight.astype(jnp.float32)), axis=(1, 2)))
    tensor_max = lax.optimization_barrier(jnp.max(jnp.where(tensor_id[None, :] == tensor_range[:, None], block_peak[None, :], 0.0), axis=1))
    block_scale = lax.optimization_barrier(jnp.sum(jnp.where(tensor_id[:, None] == tensor_range[None, :], tensor_max[None, :], 0.0), axis=1))
    recast = new_weight.astype(jnp.float32) / (block_scale + small_eps)[:, None, None]
    return recast.astype(jnp.bfloat16)
```

```python
import functools
import math

import jax
import jax.numpy as jnp
from jax import lax
from jax.experimental import pallas as pl
from jax.experimental.pallas import tpu as pltpu
from jax.sharding import PartitionSpec as P

BS = 1024
GB = 36
HALF = 18
NX, NZ, NY = 4, 8, 8
SLOTS = NZ * NY
ROWS = 16
CH = 4
W = BS // CH
PADB = 40

learn_rate = 0.02
small_eps = 1e-06
f32 = jnp.float32
bf16 = jnp.bfloat16
MESH = pl.DeviceIdType.MESH


def kernel(
    chosen, dkey, ownmat, grads, factors, weights, out,
    gin, fac, win, xa, xs, xb, summed, zsend, zrcv, gbuf, acc, rp, pbuf, yrcv, fin,
    gsq, psq, sc, bmax, sty, stz, stx, mxy, mxz, mxx,
    in_sem, xsnd, xrcv, zsnd, zrs, ysnd, yrs, csnd, crs, dsnd, drs, st_snd, st_rcv,
):
    g = lax.axis_index("dp")
    f = lax.axis_index("fsdp")
    z = lax.div(f, NY)
    yc = lax.rem(f, NY)

    def xdev(d):
        return {"dp": lax.rem(g + d, NX)}

    def zdev(d):
        return {"fsdp": lax.rem(z + d, NZ) * NY + yc}

    def ydev(d):
        return {"fsdp": z * NY + lax.rem(yc + d, NY)}

    loads = [
        pltpu.make_async_copy(grads.at[:, :, pl.ds(k * W, W)], gin.at[k], in_sem.at[k])
        for k in range(CH)
    ]
    load_f = pltpu.make_async_copy(factors, fac, in_sem.at[CH])
    load_w = pltpu.make_async_copy(weights, win, in_sem.at[CH + 1])
    for c in loads:
        c.start()
    load_f.start()
    load_w.start()

    barrier = pltpu.get_barrier_semaphore()
    peers = (
        [xdev(d) for d in range(1, NX)]
        + [zdev(d) for d in range(1, NZ)]
        + [ydev(d) for d in range(1, NY)]
    )
    for p in peers:
        pl.semaphore_signal(barrier, inc=1, device_id=p, device_id_type=MESH)
    gsq[...] = jnp.zeros_like(gsq)
    psq[...] = jnp.zeros_like(psq)
    pl.semaphore_wait(barrier, len(peers))

    sends = []

    def send(src, dst, ss, rs, dev):
        c = pltpu.make_async_remote_copy(
            src_ref=src, dst_ref=dst, send_sem=ss, recv_sem=rs, device_id=dev, device_id_type=MESH
        )
        c.start()
        return c

    gnext = lax.rem(g + 1, NX) * GB
    gprev = lax.rem(g + 3, NX) * GB
    gfar = lax.rem(g + 2, NX) * GB
    gown = g * GB

    def x1(k):
        loads[k].wait()
        a = send(gin.at[k, pl.ds(gfar, HALF)], xa.at[0, k], xsnd.at[0, 0, k], xrcv.at[0, 0, k], xdev(1))
        b = send(gin.at[k, pl.ds(gfar + HALF, HALF)], xa.at[1, k], xsnd.at[0, 1, k], xrcv.at[0, 1, k], xdev(3))
        sends.extend([a, b])
        return a, b

    def x2own(k):
        a = send(
            gin.at[k, pl.ds(gnext + HALF, HALF)], xb.at[0, k, pl.ds(HALF, HALF)],
            xsnd.at[1, 0, k], xrcv.at[1, 0, k], xdev(1),
        )
        b = send(
            gin.at[k, pl.ds(gprev, HALF)], xb.at[1, k, pl.ds(0, HALF)],
            xsnd.at[1, 1, k], xrcv.at[1, 1, k], xdev(3),
        )
        sends.extend([a, b])
        return a, b

    def x2sum(k, first):
        out_c = []
        for side, base in ((0, gnext), (1, gprev + HALF)):
            first[side].wait_recv()

            @pl.loop(0, HALF, unroll=3)
            def _(i):
                xs[side, k, i] = (gin[k, base + i].astype(f32) + xa[side, k, i].astype(f32)).astype(bf16)

            at = pl.ds(0, HALF) if side == 0 else pl.ds(HALF, HALF)
            out_c.append(
                send(
                    xs.at[side, k], xb.at[side, k, at],
                    xsnd.at[2, side, k], xrcv.at[2, side, k], xdev(1 if side == 0 else 3),
                )
            )
        sends.extend(out_c)
        return out_c

    def pack_and_z(k, got):
        for c in got:
            c.wait_recv()

        @pl.loop(0, GB, unroll=4)
        def _(b):
            v = gin[k, gown + b].astype(f32) + xb[0, k, b].astype(f32) + xb[1, k, b].astype(f32)
            summed[k][b] = v.astype(bf16)

        @pl.loop(0, SLOTS, unroll=8)
        def _(o):
            zsend[k, o] = summed[k][chosen[o]]

        for d in (4, 3, 5, 2, 6, 1, 7):
            tz = lax.rem(z + d, NZ)
            sends.append(
                send(zsend.at[k, pl.ds(tz * NY, NY)], zrcv.at[k, z], zsnd.at[d, k], zrs.at[k], zdev(d))
            )
        zrcv[k, z] = zsend[k, pl.ds(z * NY, NY)]

    def wait_all(buf, k, sem):
        part = buf.at[pl.ds(0, 7)] if k is None else buf.at[k, pl.ds(0, 7)]
        pltpu.make_async_copy(part, part, sem if k is None else sem.at[k]).wait()

    def z_to_y(k):
        wait_all(zrcv, k, zrs)
        for d in (4, 3, 5, 2, 6, 1, 7):
            q = lax.rem(yc + d, NY)
            sends.append(send(zrcv.at[k, :, q], gbuf.at[k, :, yc], ysnd.at[d, k], yrs.at[k], ydev(d)))
        gbuf[k, :, yc] = zrcv[k, :, yc]

    def mul_right(k):
        wait_all(gbuf, k, yrs)
        if k == 0:
            load_f.wait()

        @pl.loop(0, 4)
        def _(i):
            part = gbuf[k, pl.ds(i * 2, 2)].reshape(256, W)
            wide = part.astype(f32)
            gsq[...] += jnp.sum((wide * wide).reshape(32, 8, W), axis=0)
            prod = jnp.dot(part, fac[1, pl.ds(k * W, W), :], preferred_element_type=f32)
            rows = pl.ds(pl.multiple_of(i * 256, 256), 256)
            if k > 0:
                prod = prod + acc[rows, :]
            if k == CH - 1:
                rp[rows, :] = prod.astype(bf16)
            else:
                acc[rows, :] = prod

    x1s, x2s = {}, {}
    x1s[0] = x1(0)
    x2s[0] = list(x2own(0))
    x1s[1] = x1(1)
    for t in range(CH + 4):
        if t < CH:
            x2s[t] += x2sum(t, x1s[t])
            if t + 1 < CH:
                x2s[t + 1] = list(x2own(t + 1))
            if t + 2 < CH:
                x1s[t + 2] = x1(t + 2)
        if 0 <= t - 1 < CH:
            pack_and_z(t - 1, x2s[t - 1])
        if 0 <= t - 3 < CH:
            z_to_y(t - 3)
        if 0 <= t - 4 < CH:
            mul_right(t - 4)

    def mul_left(j):
        @pl.loop(0, 4)
        def _(i):
            rows = pl.ds(pl.multiple_of(i * 256, 256), 256)
            prod = jnp.dot(fac[0, rows, :], rp[:, pl.ds(j * W, W)], preferred_element_type=f32)
            psq[...] += jnp.sum((prod * prod).reshape(32, 8, W), axis=0)
            pbuf[j, pl.ds(i * 2, 2)] = prod.astype(bf16).reshape(2, NY, ROWS, W)

        for d in (4, 3, 5, 2, 6, 1, 7):
            q = lax.rem(yc + d, NY)
            sends.append(send(pbuf.at[j, :, q], yrcv.at[j, yc], csnd.at[d, j], crs.at[j], ydev(d)))
        yrcv[j, yc] = pbuf[j, :, yc]

    def y_to_z(j):
        wait_all(yrcv, j, crs)
        for d in (4, 3, 5, 2, 6, 1, 7):
            tz = lax.rem(z + d, NZ)
            sends.append(send(yrcv.at[j, :, tz], fin[j].at[z], dsnd.at[d, j], drs.at[j], zdev(d)))
        fin[j][z] = yrcv[j, :, z]

    def exchange(buf, value, me, count, dev, row):
        buf[me] = value
        got = []
        for d in range(1, count):
            c = send(buf.at[me], buf.at[me], st_snd.at[row, d], st_rcv.at[row, d], dev(d))
            got.append(c)
        sends.extend(got)
        for c in got:
            c.wait_recv()

    for j in range(CH + 1):
        if j < CH:
            mul_left(j)
        if j > 0:
            y_to_z(j - 1)

    lane = lax.broadcasted_iota(jnp.int32, (8, 128), 1)
    sub = lax.broadcasted_iota(jnp.int32, (8, 128), 0)
    hot = ownmat[...] == lax.broadcasted_iota(jnp.int32, (PADB, 128), 1)
    used = jnp.sum(jnp.where(hot, 1.0, 0.0), axis=0, keepdims=True)
    gtot = jnp.sum(gsq[...], keepdims=True)
    ptot = jnp.sum(psq[...], keepdims=True)
    mine = jnp.where(sub == 0, gtot * used, jnp.where(sub == 1, ptot, 0.0))
    exchange(sty, jnp.where(lane == f, mine, 0.0), yc, NY, ydev, 0)
    exchange(stz, jnp.sum(sty[...], axis=0), z, NZ, zdev, 1)
    plane = jnp.sum(stz[...], axis=0)
    exchange(stx, plane, g, NX, xdev, 2)
    squares = jnp.sum(jnp.sum(stx[...], axis=0)[0:1, :], axis=1, keepdims=True)
    scale = 0.5 * math.sqrt(float(NX * GB * BS * BS)) / jnp.sqrt(squares)
    count = float(BS * BS)
    ratio = jnp.sqrt((plane[0:1, :] / count + small_eps) / (plane[1:2, :] / count + small_eps))
    per_block = jnp.sum(jnp.where(hot, scale * ratio, 0.0), axis=1, keepdims=True)
    sc[...] = jnp.broadcast_to(per_block, (PADB, W))
    bmax[...] = jnp.zeros_like(bmax)
    load_w.wait()

    for j in range(CH):
        wait_all(fin[j], None, drs.at[j])
        cols = pl.ds(j * W, W)

        @pl.loop(0, GB, unroll=4)
        def _(b):
            o = dkey[b]
            u = fin[j][lax.div(o, NY), lax.rem(o, NY)].astype(f32)
            upd = (sc[pl.ds(b, 1), :] * u).astype(bf16).astype(f32)
            nw = (win[b, :, cols].astype(f32) - learn_rate * upd).astype(bf16)
            out[b, :, cols] = nw
            mag = jnp.abs(nw.astype(f32))
            mag = jnp.maximum(mag[0:8], mag[8:16])
            m = bmax[b]
            for s in range(W // 128):
                m = jnp.maximum(m, mag[:, s * 128 : (s + 1) * 128])
            bmax[b] = m

    bid = lax.broadcasted_iota(jnp.int32, (GB, 8, 128), 0) + g * GB
    peak = bmax[...]
    tile = jnp.zeros((8, 128), f32)
    edges = (0, 64, 72, 80, 144)
    for t in range(4):
        inside = (bid >= edges[t]) & (bid < edges[t + 1])
        m = jnp.max(jnp.max(jnp.where(inside, peak, 0.0), axis=0), axis=0, keepdims=True)
        tile = jnp.where(sub == t, m, tile)
    exchange(mxy, tile, yc, NY, ydev, 3)
    exchange(mxz, jnp.max(mxy[...], axis=0), z, NZ, zdev, 4)
    exchange(mxx, jnp.max(mxz[...], axis=0), g, NX, xdev, 5)
    top = 1.0 / (jnp.max(jnp.max(mxx[...], axis=0), axis=1, keepdims=True) + small_eps)
    rid = lax.broadcasted_iota(jnp.int32, (PADB, W), 0) + g * GB
    inv = jnp.zeros((PADB, W), f32)
    for t in range(4):
        inside = (rid >= edges[t]) & (rid < edges[t + 1])
        inv = jnp.where(inside, top[t : t + 1, :], inv)
    sc[...] = inv

    @pl.loop(0, GB, unroll=2)
    def _(b):
        s = sc[pl.ds(b, 1), :]
        for c in range(CH):
            at = pl.ds(c * W, W)
            out[b, :, at] = (out[b, :, at].astype(f32) * s).astype(bf16)

    for c in sends:
        c.wait_send()


def per_device(grad_parts, factors, weights, block_owner):
    group = lax.axis_index("dp")
    owners = lax.dynamic_slice_in_dim(block_owner, group * GB, GB)
    ids = jnp.arange(GB, dtype=jnp.int32)
    slots = jnp.arange(SLOTS, dtype=jnp.int32)
    chosen = jnp.sum(jnp.where(owners[None, :] == slots[:, None], ids[None, :], 0), axis=1)
    padded = jnp.concatenate([owners, jnp.full((PADB - GB,), -1, jnp.int32)])
    ownmat = jnp.broadcast_to(padded[:, None], (PADB, 128))
    smem = pl.BlockSpec(memory_space=pltpu.SMEM)
    vmem = pl.BlockSpec(memory_space=pltpu.VMEM)
    hbm = pl.BlockSpec(memory_space=pl.ANY)
    dma = pltpu.SemaphoreType.DMA
    return pl.pallas_call(
        kernel,
        out_shape=jax.ShapeDtypeStruct((GB, ROWS, BS), bf16),
        in_specs=[smem, smem, vmem, hbm, hbm, hbm],
        out_specs=vmem,
        scratch_shapes=[
            pltpu.VMEM((CH, NX * GB, ROWS, W), bf16),
            pltpu.VMEM((2, BS, BS), bf16),
            pltpu.VMEM((GB, ROWS, BS), bf16),
            pltpu.VMEM((2, CH, HALF, ROWS, W), bf16),
            pltpu.VMEM((2, CH, HALF, ROWS, W), bf16),
            pltpu.VMEM((2, CH, GB, ROWS, W), bf16),
            [pltpu.VMEM((GB, ROWS, W), bf16)] * CH,
            pltpu.VMEM((CH, SLOTS, ROWS, W), bf16),
            pltpu.VMEM((CH, NZ, NY, ROWS, W), bf16),
            pltpu.VMEM((CH, NZ, NY, ROWS, W), bf16),
            pltpu.VMEM((BS, BS), f32),
            pltpu.VMEM((BS, BS), bf16),
            pltpu.VMEM((CH, NZ, NY, ROWS, W), bf16),
            pltpu.VMEM((CH, NY, NZ, ROWS, W), bf16),
            [pltpu.VMEM((NZ, NY, ROWS, W), bf16)] * CH,
            pltpu.VMEM((8, W), f32),
            pltpu.VMEM((8, W), f32),
            pltpu.VMEM((PADB, W), f32),
            pltpu.VMEM((GB, 8, 128), f32),
            pltpu.VMEM((NY, 8, 128), f32),
            pltpu.VMEM((NZ, 8, 128), f32),
            pltpu.VMEM((NX, 8, 128), f32),
            pltpu.VMEM((NY, 8, 128), f32),
            pltpu.VMEM((NZ, 8, 128), f32),
            pltpu.VMEM((NX, 8, 128), f32),
            dma((CH + 2,)),
            dma((3, 2, CH)),
            dma((3, 2, CH)),
            dma((8, CH)),
            dma((CH,)),
            dma((8, CH)),
            dma((CH,)),
            dma((8, CH)),
            dma((CH,)),
            dma((8, CH)),
            dma((CH,)),
            dma((6, 8)),
            dma((6, 8)),
        ],
        compiler_params=pltpu.CompilerParams(
            collective_id=0, has_side_effects=True, vmem_limit_bytes=56 * 2**20
        ),
        cost_estimate=pl.CostEstimate(flops=4 * BS**3, bytes_accessed=12 * 2**20, transcendentals=0),
        name="shampoo_step",
    )(chosen, owners, ownmat, grad_parts[0], factors.reshape(2, BS, BS), weights)


def solution(mesh):
    placed = (
        P("dp", None, "fsdp", None),
        P("dp", "fsdp", None, None, None, None),
        P("dp", "fsdp", None),
        P(),
    )
    return jax.shard_map(
        per_device, mesh=mesh, in_specs=placed, out_specs=P("dp", "fsdp", None), check_vma=False
    )
```

```python
import functools
import math

import jax
import jax.numpy as jnp
from jax import lax
from jax.experimental import pallas as pl
from jax.experimental.pallas import tpu as pltpu
from jax.sharding import PartitionSpec as P

BS = 1024
GB = 36
HALF = 18
NX, NZ, NY, NC = 4, 8, 4, 2
PAIRS = NZ * NY
SLOTS = PAIRS * NC
ROWS = 16
CH = 8
W = BS // CH
PADB = 40

learn_rate = 0.02
small_eps = 1e-06
f32 = jnp.float32
bf16 = jnp.bfloat16
MESH = pl.DeviceIdType.MESH


def kernel(
    owner, grads, factors, weights, out, inv_out,
    gin, fac, win, xa, xs, xb, summed, zsend, zrcv, gbuf, acc, rp, pbuf, yrcv, fin,
    gsq, psq, sc, bmax, sta, stb, mxa, mxb,
    ownmat, chosen_v, chosen, in_sem, xsnd, xrcv, zsnd, zrs, ysnd, yrs, csnd, crs, dsnd, drs,
    ea_snd, ea_rcv, eb_snd, eb_rcv,
):
    g = lax.axis_index("dp")
    f = lax.axis_index("fsdp")
    pair = lax.div(f, NC)
    core = lax.rem(f, NC)
    other = 1 - core

    def xdev(d):
        return {"dp": lax.rem(g + d, NX)}

    def xcdev(d):
        x = lax.rem(g + d // NC, NX)
        c = lax.rem(core + d % NC, NC)
        return {"dp": x, "fsdp": pair * NC + c}

    def pair_at(d):
        z = lax.rem(lax.div(pair, NY) + lax.div(d, NY), NZ)
        y = lax.rem(lax.rem(pair, NY) + lax.rem(d, NY), NY)
        return z * NY + y

    swap = {"fsdp": pair * NC + other}

    loads = [
        pltpu.make_async_copy(grads.at[:, :, pl.ds(k * W, W)], gin.at[k], in_sem.at[k])
        for k in range(CH)
    ]
    load_f = pltpu.make_async_copy(factors, fac, in_sem.at[CH])
    load_w = pltpu.make_async_copy(weights, win, in_sem.at[CH + 1])
    for c in loads:
        c.start()
    load_f.start()
    load_w.start()

    barrier = pltpu.get_barrier_semaphore()
    for d in range(1, NX * NC):
        pl.semaphore_signal(barrier, inc=1, device_id=xcdev(d), device_id_type=MESH)

    @pl.loop(1, PAIRS)
    def _(d):
        pl.semaphore_signal(
            barrier, inc=1, device_id={"fsdp": pair_at(d) * NC + core}, device_id_type=MESH
        )

    ownmat[...] = jnp.full((PADB, 128), -1, jnp.int32)
    for b in range(GB):
        ownmat[pl.ds(b, 1), :] = jnp.full((1, 128), owner[g * GB + b], jnp.int32)
    hot = ownmat[...] == lax.broadcasted_iota(jnp.int32, (PADB, 128), 1)
    picked = jnp.where(hot, lax.broadcasted_iota(jnp.int32, (PADB, 128), 0), 0)
    chosen_v[...] = jnp.broadcast_to(jnp.max(picked, axis=0, keepdims=True), (8, 128))
    load_c = pltpu.make_async_copy(chosen_v, chosen, in_sem.at[CH + 2])
    load_c.start()
    gsq[...] = jnp.zeros_like(gsq)
    psq[...] = jnp.zeros_like(psq)
    pl.semaphore_wait(barrier, NX * NC - 1 + PAIRS - 1)
    load_c.wait()

    sends = []

    def send(src, dst, ss, rs, dev):
        c = pltpu.make_async_remote_copy(
            src_ref=src, dst_ref=dst, send_sem=ss, recv_sem=rs, device_id=dev, device_id_type=MESH
        )
        c.start()
        return c

    gnext = lax.rem(g + 1, NX) * GB
    gprev = lax.rem(g + 3, NX) * GB
    gfar = lax.rem(g + 2, NX) * GB
    gown = g * GB

    def x1(k):
        loads[k].wait()
        a = send(gin.at[k, pl.ds(gfar, HALF)], xa.at[0, k], xsnd.at[0, 0, k], xrcv.at[0, 0, k], xdev(1))
        b = send(gin.at[k, pl.ds(gfar + HALF, HALF)], xa.at[1, k], xsnd.at[0, 1, k], xrcv.at[0, 1, k], xdev(3))
        sends.extend([a, b])
        return a, b

    def x2own(k):
        a = send(
            gin.at[k, pl.ds(gnext + HALF, HALF)], xb.at[0, k, pl.ds(HALF, HALF)],
            xsnd.at[1, 0, k], xrcv.at[1, 0, k], xdev(1),
        )
        b = send(
            gin.at[k, pl.ds(gprev, HALF)], xb.at[1, k, pl.ds(0, HALF)],
            xsnd.at[1, 1, k], xrcv.at[1, 1, k], xdev(3),
        )
        sends.extend([a, b])
        return a, b

    def x2sum(k, first):
        out_c = []
        for side, base in ((0, gnext), (1, gprev + HALF)):
            first[side].wait_recv()

            @pl.loop(0, HALF, unroll=3)
            def _(i):
                xs[side, k, i] = (gin[k, base + i].astype(f32) + xa[side, k, i].astype(f32)).astype(bf16)

            at = pl.ds(0, HALF) if side == 0 else pl.ds(HALF, HALF)
            out_c.append(
                send(
                    xs.at[side, k], xb.at[side, k, at],
                    xsnd.at[2, side, k], xrcv.at[2, side, k], xdev(1 if side == 0 else 3),
                )
            )
        sends.extend(out_c)
        return out_c

    def spread(src, dst, ss, rs):
        @pl.loop(1, PAIRS)
        def _(d):
            to = pair_at(d)
            send(src.at[to], dst.at[pair], ss, rs, {"fsdp": to * NC + core})

    def pack_and_z(k, got):
        for c in got:
            c.wait_recv()

        @pl.loop(0, GB, unroll=4)
        def _(b):
            v = gin[k, gown + b].astype(f32) + xb[0, k, b].astype(f32) + xb[1, k, b].astype(f32)
            summed[k][b] = v.astype(bf16)

        @pl.loop(0, PAIRS, unroll=4)
        def _(p):
            for c in range(NC):
                zsend[k, p, c] = summed[k][chosen[0, p * NC + c]]

        spread(zsend.at[k], zrcv.at[k], zsnd.at[k], zrs.at[k])
        zrcv[k, pair] = zsend[k, pair]

    def wait_all(buf, sem):
        part = buf.at[pl.ds(0, PAIRS - 1)]
        pltpu.make_async_copy(part, part, sem).wait()

    swaps = {}

    def z_to_y(k):
        wait_all(zrcv.at[k], zrs.at[k])
        swaps[k] = send(zrcv.at[k, :, other], gbuf.at[k, :, core], ysnd.at[k], yrs.at[k], swap)
        gbuf[k, :, core] = zrcv[k, :, core]

    def mul_right(k):
        swaps[k].wait()
        if k == 0:
            load_f.wait()

        @pl.loop(0, 4)
        def _(i):
            part = gbuf[k, pl.ds(i * 8, 8)].reshape(256, W)
            wide = part.astype(f32)
            gsq[...] += jnp.sum((wide * wide).reshape(32, 8, W), axis=0)
            prod = jnp.dot(part, fac[1, pl.ds(k * W, W), :], preferred_element_type=f32)
            rows = pl.ds(pl.multiple_of(i * 256, 256), 256)
            if k > 0:
                prod = prod + acc[rows, :]
            if k == CH - 1:
                rp[rows, :] = prod.astype(bf16)
            else:
                acc[rows, :] = prod

    x1s, x2s = {}, {}
    x1s[0] = x1(0)
    x2s[0] = list(x2own(0))
    x1s[1] = x1(1)
    for t in range(CH + 4):
        if t < CH:
            x2s[t] += x2sum(t, x1s[t])
            if t + 1 < CH:
                x2s[t + 1] = list(x2own(t + 1))
            if t + 2 < CH:
                x1s[t + 2] = x1(t + 2)
        if 0 <= t - 1 < CH:
            pack_and_z(t - 1, x2s[t - 1])
        if 0 <= t - 3 < CH:
            z_to_y(t - 3)
        if 0 <= t - 4 < CH:
            mul_right(t - 4)

    def mul_left(j):
        @pl.loop(0, 4)
        def _(i):
            rows = pl.ds(pl.multiple_of(i * 256, 256), 256)
            prod = jnp.dot(fac[0, rows, :], rp[:, pl.ds(j * W, W)], preferred_element_type=f32)
            psq[...] += jnp.sum((prod * prod).reshape(32, 8, W), axis=0)
            pbuf[j, pl.ds(i * 8, 8)] = prod.astype(bf16).reshape(8, NC, ROWS, W)

        spread(pbuf.at[j], yrcv.at[j], csnd.at[j], crs.at[j])
        yrcv[j, pair] = pbuf[j, pair]

    def y_to_z(j):
        wait_all(yrcv.at[j], crs.at[j])
        swaps[j] = send(yrcv.at[j, :, other], fin[j].at[:, core], dsnd.at[j], drs.at[j], swap)
        fin[j][:, core] = yrcv[j, :, core]

    def exchange(buf_a, buf_b, value, merge, row):
        me = g * NC + core
        buf_a[me] = value
        got = [
            send(buf_a.at[me], buf_a.at[me], ea_snd.at[row, d], ea_rcv.at[row, d], xcdev(d))
            for d in range(1, NX * NC)
        ]
        sends.extend(got)
        for c in got:
            c.wait_recv()
        buf_b[pair] = merge(buf_a[...])

        @pl.loop(1, PAIRS)
        def _(d):
            to = pair_at(d)
            send(buf_b.at[pair], buf_b.at[pair], eb_snd.at[row], eb_rcv.at[row], {"fsdp": to * NC + core})

        wait_all(buf_b, eb_rcv.at[row])

    for j in range(CH):
        mul_left(j)

    lane = lax.broadcasted_iota(jnp.int32, (8, 128), 1)
    sub = lax.broadcasted_iota(jnp.int32, (8, 128), 0)
    used = jnp.sum(jnp.where(hot, 1.0, 0.0), axis=0, keepdims=True)
    gtot = jnp.sum(gsq[...], keepdims=True)
    ptot = jnp.sum(psq[...], keepdims=True)
    mine = jnp.where(sub == 0, gtot * used, jnp.where(sub == 1, ptot, 0.0))
    lead = lax.broadcasted_iota(jnp.int32, (NX * NC, 8, 128), 0)

    def merge(t):
        plane = jnp.sum(jnp.where(lax.div(lead, NC) == g, t, 0.0), axis=0)
        return jnp.where(sub == 2, jnp.sum(t, axis=0)[0:1, :], plane)

    exchange(sta, stb, jnp.where(lane == f, mine, 0.0), merge, 0)
    for j in range(CH):
        y_to_z(j)
    plane = jnp.sum(stb[...], axis=0)
    squares = jnp.sum(plane[2:3, :], axis=1, keepdims=True)
    scale = 0.5 * math.sqrt(float(NX * GB * BS * BS)) / jnp.sqrt(squares)
    count = float(BS * BS)
    ratio = jnp.sqrt((plane[0:1, :] / count + small_eps) / (plane[1:2, :] / count + small_eps))
    per_block = jnp.sum(jnp.where(hot, scale * ratio, 0.0), axis=1, keepdims=True)
    sc[...] = jnp.broadcast_to(per_block, (PADB, W))
    bmax[...] = jnp.zeros_like(bmax)
    load_w.wait()

    for j in range(CH):
        swaps[j].wait_recv()
        cols = pl.ds(j * W, W)

        @pl.loop(0, GB, unroll=4)
        def _(b):
            o = owner[g * GB + b]
            u = fin[j][lax.div(o, NC), lax.rem(o, NC)].astype(f32)
            upd = (sc[pl.ds(b, 1), :] * u).astype(bf16).astype(f32)
            nw = (win[b, :, cols].astype(f32) - learn_rate * upd).astype(bf16)
            out[b, :, cols] = nw
            mag = jnp.abs(nw.astype(f32))
            mag = jnp.maximum(mag[0:8], mag[8:16])
            m = bmax[b]
            for s in range(W // 128):
                m = jnp.maximum(m, mag[:, s * 128 : (s + 1) * 128])
            bmax[b] = m

    bid = lax.broadcasted_iota(jnp.int32, (GB, 8, 128), 0) + g * GB
    peak = bmax[...]
    tile = jnp.zeros((8, 128), f32)
    edges = (0, 64, 72, 80, 144)
    for t in range(4):
        inside = (bid >= edges[t]) & (bid < edges[t + 1])
        m = jnp.max(jnp.max(jnp.where(inside, peak, 0.0), axis=0), axis=0, keepdims=True)
        tile = jnp.where(sub == t, m, tile)
    exchange(mxa, mxb, tile, lambda t: jnp.max(t, axis=0), 1)
    scale = 1.0 / (jnp.max(jnp.max(mxb[...], axis=0), axis=1, keepdims=True) + small_eps)
    rid = lax.broadcasted_iota(jnp.int32, (PADB, 128), 0) + g * GB
    inv = jnp.zeros((PADB, 128), f32)
    for t in range(4):
        inside = (rid >= edges[t]) & (rid < edges[t + 1])
        inv = jnp.where(inside, scale[t : t + 1, :], inv)
    inv_out[...] = inv

    for c in sends:
        c.wait_send()
    for k in range(CH):
        wait_all(zsend.at[k], zsnd.at[k])
        wait_all(pbuf.at[k], csnd.at[k])
        swaps[k].wait_send()
    for row, buf in ((0, stb), (1, mxb)):
        wait_all(buf, eb_snd.at[row])


def per_device(grad_parts, factors, weights, block_owner):
    smem = pl.BlockSpec(memory_space=pltpu.SMEM)
    vmem = pl.BlockSpec(memory_space=pltpu.VMEM)
    hbm = pl.BlockSpec(memory_space=pl.ANY)
    dma = pltpu.SemaphoreType.DMA
    new_weight, inv = pl.pallas_call(
        kernel,
        out_shape=(jax.ShapeDtypeStruct((GB, ROWS, BS), bf16), jax.ShapeDtypeStruct((PADB, 128), f32)),
        in_specs=[smem, hbm, hbm, hbm],
        out_specs=(vmem, vmem),
        scratch_shapes=[
            pltpu.VMEM((CH, NX * GB, ROWS, W), bf16),
            pltpu.VMEM((2, BS, BS), bf16),
            pltpu.VMEM((GB, ROWS, BS), bf16),
            pltpu.VMEM((2, CH, HALF, ROWS, W), bf16),
            pltpu.VMEM((2, CH, HALF, ROWS, W), bf16),
            pltpu.VMEM((2, CH, GB, ROWS, W), bf16),
            [pltpu.VMEM((GB, ROWS, W), bf16)] * CH,
            pltpu.VMEM((CH, PAIRS, NC, ROWS, W), bf16),
            pltpu.VMEM((CH, PAIRS, NC, ROWS, W), bf16),
            pltpu.VMEM((CH, PAIRS, NC, ROWS, W), bf16),
            pltpu.VMEM((BS, BS), f32),
            pltpu.VMEM((BS, BS), bf16),
            pltpu.VMEM((CH, PAIRS, NC, ROWS, W), bf16),
            pltpu.VMEM((CH, PAIRS, NC, ROWS, W), bf16),
            [pltpu.VMEM((PAIRS, NC, ROWS, W), bf16)] * CH,
            pltpu.VMEM((8, W), f32),
            pltpu.VMEM((8, W), f32),
            pltpu.VMEM((PADB, W), f32),
            pltpu.VMEM((GB, 8, 128), f32),
            pltpu.VMEM((NX * NC, 8, 128), f32),
            pltpu.VMEM((PAIRS, 8, 128), f32),
            pltpu.VMEM((NX * NC, 8, 128), f32),
            pltpu.VMEM((PAIRS, 8, 128), f32),
            pltpu.VMEM((PADB, 128), jnp.int32),
            pltpu.VMEM((8, 128), jnp.int32),
            pltpu.SMEM((8, 128), jnp.int32),
            dma((CH + 3,)),
            dma((3, 2, CH)),
            dma((3, 2, CH)),
            dma((CH,)),
            dma((CH,)),
            dma((CH,)),
            dma((CH,)),
            dma((CH,)),
            dma((CH,)),
            dma((CH,)),
            dma((CH,)),
            dma((2, 8)),
            dma((2, 8)),
            dma((2,)),
            dma((2,)),
        ],
        compiler_params=pltpu.CompilerParams(
            collective_id=0, has_side_effects=True, vmem_limit_bytes=56 * 2**20
        ),
        cost_estimate=pl.CostEstimate(flops=4 * BS**3, bytes_accessed=12 * 2**20, transcendentals=0),
        name="shampoo_step",
    )(block_owner, grad_parts[0], factors.reshape(2, BS, BS), weights)
    return (new_weight.astype(f32) * inv[:GB, :1, None]).astype(bf16)


def solution(mesh):
    placed = (
        P("dp", None, "fsdp", None),
        P("dp", "fsdp", None, None, None, None),
        P("dp", "fsdp", None),
        P(),
    )
    return jax.shard_map(
        per_device, mesh=mesh, in_specs=placed, out_specs=P("dp", "fsdp", None), check_vma=False
    )
```

```python
import functools
import math

import jax
import jax.numpy as jnp
from jax import lax
from jax.experimental import pallas as pl
from jax.experimental.pallas import tpu as pltpu
from jax.sharding import PartitionSpec as P

BS = 1024
GB = 36
HALF = 18
NX, NZ, NY, NC = 4, 8, 4, 2
PAIRS = NZ * NY
SLOTS = PAIRS * NC
ROWS = 16
CH = 8
W = BS // CH
CJ = 4
W2 = BS // CJ
PADB = 40

learn_rate = 0.02
small_eps = 1e-06
f32 = jnp.float32
bf16 = jnp.bfloat16
MESH = pl.DeviceIdType.MESH


def kernel(
    owner, grads, factors, weights, out, inv_out,
    gin, fac, win, xa, xs, xb, summed, zsend, zrcv, gbuf, acc, rp, pbuf, yrcv, fin,
    gsq, psq, sc, bmax, sta, stb, mxa, mxb,
    ownmat, chosen_v, chosen, in_sem, xsnd, xrcv, zsnd, zrs, ysnd, yrs, csnd, crs, dsnd, drs,
    ea_snd, ea_rcv, eb_snd, eb_rcv,
):
    g = lax.axis_index("dp")
    f = lax.axis_index("fsdp")
    pair = lax.div(f, NC)
    core = lax.rem(f, NC)
    other = 1 - core

    def xdev(d):
        return {"dp": lax.rem(g + d, NX)}

    def xcdev(d):
        x = lax.rem(g + d // NC, NX)
        c = lax.rem(core + d % NC, NC)
        return {"dp": x, "fsdp": pair * NC + c}

    def pair_at(d):
        z = lax.rem(lax.div(pair, NY) + lax.div(d, NY), NZ)
        y = lax.rem(lax.rem(pair, NY) + lax.rem(d, NY), NY)
        return z * NY + y

    swap = {"fsdp": pair * NC + other}

    loads = [
        pltpu.make_async_copy(grads.at[:, :, pl.ds(k * W, W)], gin.at[k], in_sem.at[k])
        for k in range(CH)
    ]
    load_f = pltpu.make_async_copy(factors, fac, in_sem.at[CH])
    load_w = pltpu.make_async_copy(weights, win, in_sem.at[CH + 1])
    for c in loads:
        c.start()
    load_f.start()
    load_w.start()

    barrier = pltpu.get_barrier_semaphore()
    for d in range(1, NX * NC):
        pl.semaphore_signal(barrier, inc=1, device_id=xcdev(d), device_id_type=MESH)

    @pl.loop(1, PAIRS)
    def _(d):
        pl.semaphore_signal(
            barrier, inc=1, device_id={"fsdp": pair_at(d) * NC + core}, device_id_type=MESH
        )

    ownmat[...] = jnp.full((PADB, 128), -1, jnp.int32)
    for b in range(GB):
        ownmat[pl.ds(b, 1), :] = jnp.full((1, 128), owner[g * GB + b], jnp.int32)
    hot = ownmat[...] == lax.broadcasted_iota(jnp.int32, (PADB, 128), 1)
    picked = jnp.where(hot, lax.broadcasted_iota(jnp.int32, (PADB, 128), 0), 0)
    chosen_v[...] = jnp.broadcast_to(jnp.max(picked, axis=0, keepdims=True), (8, 128))
    load_c = pltpu.make_async_copy(chosen_v, chosen, in_sem.at[CH + 2])
    load_c.start()
    gsq[...] = jnp.zeros_like(gsq)
    psq[...] = jnp.zeros_like(psq)
    pl.semaphore_wait(barrier, NX * NC - 1 + PAIRS - 1)
    load_c.wait()

    sends = []

    def send(src, dst, ss, rs, dev):
        c = pltpu.make_async_remote_copy(
            src_ref=src, dst_ref=dst, send_sem=ss, recv_sem=rs, device_id=dev, device_id_type=MESH
        )
        c.start()
        return c

    gnext = lax.rem(g + 1, NX) * GB
    gprev = lax.rem(g + 3, NX) * GB
    gfar = lax.rem(g + 2, NX) * GB
    gown = g * GB

    def x1(k):
        loads[k].wait()
        a = send(gin.at[k, pl.ds(gfar, HALF)], xa.at[0, k], xsnd.at[0, 0, k], xrcv.at[0, 0, k], xdev(1))
        b = send(gin.at[k, pl.ds(gfar + HALF, HALF)], xa.at[1, k], xsnd.at[0, 1, k], xrcv.at[0, 1, k], xdev(3))
        sends.extend([a, b])
        return a, b

    def x2own(k):
        a = send(
            gin.at[k, pl.ds(gnext + HALF, HALF)], xb.at[0, k, pl.ds(HALF, HALF)],
            xsnd.at[1, 0, k], xrcv.at[1, 0, k], xdev(1),
        )
        b = send(
            gin.at[k, pl.ds(gprev, HALF)], xb.at[1, k, pl.ds(0, HALF)],
            xsnd.at[1, 1, k], xrcv.at[1, 1, k], xdev(3),
        )
        sends.extend([a, b])
        return a, b

    def x2sum(k, first):
        out_c = []
        for side, base in ((0, gnext), (1, gprev + HALF)):
            first[side].wait_recv()

            @pl.loop(0, HALF, unroll=3)
            def _(i):
                xs[side, k, i] = (gin[k, base + i].astype(f32) + xa[side, k, i].astype(f32)).astype(bf16)

            at = pl.ds(0, HALF) if side == 0 else pl.ds(HALF, HALF)
            out_c.append(
                send(
                    xs.at[side, k], xb.at[side, k, at],
                    xsnd.at[2, side, k], xrcv.at[2, side, k], xdev(1 if side == 0 else 3),
                )
            )
        sends.extend(out_c)
        return out_c

    def spread(src, dst, ss, rs):
        @pl.loop(0, PAIRS - 1)
        def _(i):
            n = lax.div(i, NY)
            dz = NZ // 2 + (1 - 2 * lax.rem(n, 2)) * lax.div(n + 1, 2)
            to = pair_at(dz * NY + NY - 1 - lax.rem(i, NY))
            send(src.at[to], dst.at[pair], ss, rs, {"fsdp": to * NC + core})

    def pack_and_z(k, got):
        for c in got:
            c.wait_recv()

        @pl.loop(0, GB, unroll=4)
        def _(b):
            v = gin[k, gown + b].astype(f32) + xb[0, k, b].astype(f32) + xb[1, k, b].astype(f32)
            summed[k][b] = v.astype(bf16)

        @pl.loop(0, PAIRS, unroll=4)
        def _(p):
            for c in range(NC):
                zsend[k, p, c] = summed[k][chosen[0, p * NC + c]]

        spread(zsend.at[k], zrcv.at[k], zsnd.at[k], zrs.at[k])
        zrcv[k, pair] = zsend[k, pair]

    def wait_all(buf, sem):
        part = buf.at[pl.ds(0, PAIRS - 1)]
        pltpu.make_async_copy(part, part, sem).wait()

    swaps = {}

    def z_to_y(k):
        wait_all(zrcv.at[k], zrs.at[k])
        swaps[k] = send(zrcv.at[k, :, other], gbuf.at[k, :, core], ysnd.at[k], yrs.at[k], swap)
        gbuf[k, :, core] = zrcv[k, :, core]

    def mul_right(k):
        swaps[k].wait()
        if k == 0:
            load_f.wait()

        @pl.loop(0, 4)
        def _(i):
            part = gbuf[k, pl.ds(i * 8, 8)].reshape(256, W)
            wide = part.astype(f32)
            gsq[...] += jnp.sum((wide * wide).reshape(32, 8, W), axis=0)
            prod = jnp.dot(part, fac[1, pl.ds(k * W, W), :], preferred_element_type=f32)
            rows = pl.ds(pl.multiple_of(i * 256, 256), 256)
            if k > 0:
                prod = prod + acc[rows, :]
            if k == CH - 1:
                rp[rows, :] = prod.astype(bf16)
            else:
                acc[rows, :] = prod

    x1s, x2s = {}, {}
    x1s[0] = x1(0)
    x2s[0] = list(x2own(0))
    x1s[1] = x1(1)
    for t in range(CH + 4):
        if 0 <= t - 1 < CH:
            pack_and_z(t - 1, x2s[t - 1])
        if t < CH:
            x2s[t] += x2sum(t, x1s[t])
            if t + 1 < CH:
                x2s[t + 1] = list(x2own(t + 1))
            if t + 2 < CH:
                x1s[t + 2] = x1(t + 2)
        if 0 <= t - 3 < CH:
            z_to_y(t - 3)
        if 0 <= t - 4 < CH:
            mul_right(t - 4)

    def mul_left(j):
        @pl.loop(0, 4)
        def _(i):
            rows = pl.ds(pl.multiple_of(i * 256, 256), 256)
            prod = jnp.dot(fac[0, rows, :], rp[:, pl.ds(j * W2, W2)], preferred_element_type=f32)
            psq[...] += jnp.sum((prod * prod).reshape(32, 8, W2), axis=0)
            pbuf[j, pl.ds(i * 8, 8)] = prod.astype(bf16).reshape(8, NC, ROWS, W2)

        spread(pbuf.at[j], yrcv.at[j], csnd.at[j], crs.at[j])
        yrcv[j, pair] = pbuf[j, pair]

    def y_to_z(j):
        wait_all(yrcv.at[j], crs.at[j])
        swaps[j] = send(yrcv.at[j, :, other], fin[j].at[:, core], dsnd.at[j], drs.at[j], swap)
        fin[j][:, core] = yrcv[j, :, core]

    def exchange(buf_a, buf_b, value, merge, row):
        me = g * NC + core
        buf_a[me] = value
        got = [
            send(buf_a.at[me], buf_a.at[me], ea_snd.at[row, d], ea_rcv.at[row, d], xcdev(d))
            for d in range(1, NX * NC)
        ]
        sends.extend(got)
        for c in got:
            c.wait_recv()
        buf_b[pair] = merge(buf_a[...])

        @pl.loop(1, PAIRS)
        def _(d):
            to = pair_at(d)
            send(buf_b.at[pair], buf_b.at[pair], eb_snd.at[row], eb_rcv.at[row], {"fsdp": to * NC + core})

        wait_all(buf_b, eb_rcv.at[row])

    for j in range(CJ):
        mul_left(j)

    lane = lax.broadcasted_iota(jnp.int32, (8, 128), 1)
    sub = lax.broadcasted_iota(jnp.int32, (8, 128), 0)
    used = jnp.sum(jnp.where(hot, 1.0, 0.0), axis=0, keepdims=True)
    gtot = jnp.sum(gsq[...], keepdims=True)
    ptot = jnp.sum(psq[...], keepdims=True)
    mine = jnp.where(sub == 0, gtot * used, jnp.where(sub == 1, ptot, 0.0))
    lead = lax.broadcasted_iota(jnp.int32, (NX * NC, 8, 128), 0)

    def merge(t):
        plane = jnp.sum(jnp.where(lax.div(lead, NC) == g, t, 0.0), axis=0)
        return jnp.where(sub == 2, jnp.sum(t, axis=0)[0:1, :], plane)

    exchange(sta, stb, jnp.where(lane == f, mine, 0.0), merge, 0)
    for j in range(CJ):
        y_to_z(j)
    plane = jnp.sum(stb[...], axis=0)
    squares = jnp.sum(plane[2:3, :], axis=1, keepdims=True)
    scale = 0.5 * math.sqrt(float(NX * GB * BS * BS)) / jnp.sqrt(squares)
    count = float(BS * BS)
    ratio = jnp.sqrt((plane[0:1, :] / count + small_eps) / (plane[1:2, :] / count + small_eps))
    per_block = jnp.sum(jnp.where(hot, scale * ratio, 0.0), axis=1, keepdims=True)
    sc[...] = jnp.broadcast_to(per_block, (PADB, W2))
    bmax[...] = jnp.zeros_like(bmax)
    load_w.wait()

    for j in range(CJ):
        swaps[j].wait_recv()
        cols = pl.ds(j * W2, W2)

        @pl.loop(0, GB, unroll=4)
        def _(b):
            o = owner[g * GB + b]
            u = fin[j][lax.div(o, NC), lax.rem(o, NC)].astype(f32)
            upd = (sc[pl.ds(b, 1), :] * u).astype(bf16).astype(f32)
            nw = (win[b, :, cols].astype(f32) - learn_rate * upd).astype(bf16)
            out[b, :, cols] = nw
            mag = jnp.abs(nw.astype(f32))
            mag = jnp.maximum(mag[0:8], mag[8:16])
            m = bmax[b]
            for s in range(W2 // 128):
                m = jnp.maximum(m, mag[:, s * 128 : (s + 1) * 128])
            bmax[b] = m

    bid = lax.broadcasted_iota(jnp.int32, (GB, 8, 128), 0) + g * GB
    peak = bmax[...]
    tile = jnp.zeros((8, 128), f32)
    edges = (0, 64, 72, 80, 144)
    for t in range(4):
        inside = (bid >= edges[t]) & (bid < edges[t + 1])
        m = jnp.max(jnp.max(jnp.where(inside, peak, 0.0), axis=0), axis=0, keepdims=True)
        tile = jnp.where(sub == t, m, tile)
    exchange(mxa, mxb, tile, lambda t: jnp.max(t, axis=0), 1)
    scale = 1.0 / (jnp.max(jnp.max(mxb[...], axis=0), axis=1, keepdims=True) + small_eps)
    rid = lax.broadcasted_iota(jnp.int32, (PADB, 128), 0) + g * GB
    inv = jnp.zeros((PADB, 128), f32)
    for t in range(4):
        inside = (rid >= edges[t]) & (rid < edges[t + 1])
        inv = jnp.where(inside, scale[t : t + 1, :], inv)
    inv_out[...] = inv

    for c in sends:
        c.wait_send()
    for k in range(CH):
        wait_all(zsend.at[k], zsnd.at[k])
    for k in range(CJ):
        wait_all(pbuf.at[k], csnd.at[k])
        swaps[k].wait_send()
    for row, buf in ((0, stb), (1, mxb)):
        wait_all(buf, eb_snd.at[row])


def rescale(weight, inv, out):
    @pl.loop(0, GB, unroll=4)
    def _(b):
        s = inv[pl.ds(b, 1), :]
        for c in range(BS // 128):
            at = pl.ds(c * 128, 128)
            out[b, :, at] = (weight[b, :, at].astype(f32) * s).astype(bf16)


def per_device(grad_parts, factors, weights, block_owner):
    smem = pl.BlockSpec(memory_space=pltpu.SMEM)
    vmem = pl.BlockSpec(memory_space=pltpu.VMEM)
    hbm = pl.BlockSpec(memory_space=pl.ANY)
    dma = pltpu.SemaphoreType.DMA
    new_weight, inv = pl.pallas_call(
        kernel,
        out_shape=(jax.ShapeDtypeStruct((GB, ROWS, BS), bf16), jax.ShapeDtypeStruct((PADB, 128), f32)),
        in_specs=[smem, hbm, hbm, hbm],
        out_specs=(vmem, vmem),
        scratch_shapes=[
            pltpu.VMEM((CH, NX * GB, ROWS, W), bf16),
            pltpu.VMEM((2, BS, BS), bf16),
            pltpu.VMEM((GB, ROWS, BS), bf16),
            pltpu.VMEM((2, CH, HALF, ROWS, W), bf16),
            pltpu.VMEM((2, CH, HALF, ROWS, W), bf16),
            pltpu.VMEM((2, CH, GB, ROWS, W), bf16),
            [pltpu.VMEM((GB, ROWS, W), bf16)] * CH,
            pltpu.VMEM((CH, PAIRS, NC, ROWS, W), bf16),
            pltpu.VMEM((CH, PAIRS, NC, ROWS, W), bf16),
            pltpu.VMEM((CH, PAIRS, NC, ROWS, W), bf16),
            pltpu.VMEM((BS, BS), f32),
            pltpu.VMEM((BS, BS), bf16),
            pltpu.VMEM((CJ, PAIRS, NC, ROWS, W2), bf16),
            pltpu.VMEM((CJ, PAIRS, NC, ROWS, W2), bf16),
            [pltpu.VMEM((PAIRS, NC, ROWS, W2), bf16)] * CJ,
            pltpu.VMEM((8, W), f32),
            pltpu.VMEM((8, W2), f32),
            pltpu.VMEM((PADB, W2), f32),
            pltpu.VMEM((GB, 8, 128), f32),
            pltpu.VMEM((NX * NC, 8, 128), f32),
            pltpu.VMEM((PAIRS, 8, 128), f32),
            pltpu.VMEM((NX * NC, 8, 128), f32),
            pltpu.VMEM((PAIRS, 8, 128), f32),
            pltpu.VMEM((PADB, 128), jnp.int32),
            pltpu.VMEM((8, 128), jnp.int32),
            pltpu.SMEM((8, 128), jnp.int32),
            dma((CH + 3,)),
            dma((3, 2, CH)),
            dma((3, 2, CH)),
            dma((CH,)),
            dma((CH,)),
            dma((CH,)),
            dma((CH,)),
            dma((CH,)),
            dma((CH,)),
            dma((CH,)),
            dma((CH,)),
            dma((2, 8)),
            dma((2, 8)),
            dma((2,)),
            dma((2,)),
        ],
        compiler_params=pltpu.CompilerParams(
            collective_id=0, has_side_effects=True, vmem_limit_bytes=56 * 2**20
        ),
        cost_estimate=pl.CostEstimate(flops=4 * BS**3, bytes_accessed=12 * 2**20, transcendentals=0),
        name="shampoo_step",
    )(block_owner, grad_parts[0], factors.reshape(2, BS, BS), weights)
    return pl.pallas_call(
        rescale,
        out_shape=jax.ShapeDtypeStruct((GB, ROWS, BS), bf16),
        in_specs=[vmem, vmem],
        out_specs=vmem,
        cost_estimate=pl.CostEstimate(flops=GB * ROWS * BS, bytes_accessed=3 * 2**20, transcendentals=0),
        name="rescale",
    )(new_weight, inv)


def solution(mesh):
    placed = (
        P("dp", None, "fsdp", None),
        P("dp", "fsdp", None, None, None, None),
        P("dp", "fsdp", None),
        P(),
    )
    return jax.shard_map(
        per_device, mesh=mesh, in_specs=placed, out_specs=P("dp", "fsdp", None), check_vma=False
    )
```

```python
import functools
import math

import jax
import jax.numpy as jnp
from jax import lax
from jax.experimental import pallas as pl
from jax.experimental.pallas import tpu as pltpu
from jax.sharding import PartitionSpec as P

BS = 1024
GB = 36
HALF = 18
NX, NZ, NY, NC = 4, 8, 4, 2
PAIRS = NZ * NY
SLOTS = PAIRS * NC
ROWS = 16
CH = 8
W = BS // CH
CJ = 4
W2 = BS // CJ
PADB = 40

learn_rate = 0.02
small_eps = 1e-06
f32 = jnp.float32
bf16 = jnp.bfloat16
MESH = pl.DeviceIdType.MESH


def kernel(
    owner, grads, factors, weights, out, inv_out,
    gin, fac, win, xa, xs, xb, summed, zsend, zrcv, gbuf, acc, rp, pbuf, yrcv, fin,
    gsq, psq, sc, bmax, sta, stb, mxa, mxb,
    ownmat, chosen_v, chosen, fresh, in_sem, xsnd, xrcv, zsnd, zrs, ysnd, yrs, csnd, crs, dsnd, drs,
    ea_snd, ea_rcv, eb_snd, eb_rcv,
):
    g = lax.axis_index("dp")
    f = lax.axis_index("fsdp")
    pair = lax.div(f, NC)
    core = lax.rem(f, NC)
    other = 1 - core

    def xdev(d):
        return {"dp": lax.rem(g + d, NX)}

    def xcdev(d):
        x = lax.rem(g + d // NC, NX)
        c = lax.rem(core + d % NC, NC)
        return {"dp": x, "fsdp": pair * NC + c}

    def pair_at(d):
        z = lax.rem(lax.div(pair, NY) + lax.div(d, NY), NZ)
        y = lax.rem(lax.rem(pair, NY) + lax.rem(d, NY), NY)
        return z * NY + y

    swap = {"fsdp": pair * NC + other}

    loads = [
        pltpu.make_async_copy(grads.at[:, :, pl.ds(k * W, W)], gin.at[k], in_sem.at[k])
        for k in range(CH)
    ]
    load_f = pltpu.make_async_copy(factors, fac, in_sem.at[CH])
    load_w = pltpu.make_async_copy(weights, win, in_sem.at[CH + 1])
    for c in loads:
        c.start()
    load_f.start()
    load_w.start()

    barrier = pltpu.get_barrier_semaphore()
    for d in range(1, NX * NC):
        pl.semaphore_signal(barrier, inc=1, device_id=xcdev(d), device_id_type=MESH)

    @pl.loop(1, PAIRS)
    def _(d):
        pl.semaphore_signal(
            barrier, inc=1, device_id={"fsdp": pair_at(d) * NC + core}, device_id_type=MESH
        )

    ownmat[...] = jnp.full((PADB, 128), -1, jnp.int32)
    for b in range(GB):
        ownmat[pl.ds(b, 1), :] = jnp.full((1, 128), owner[g * GB + b], jnp.int32)
    hot = ownmat[...] == lax.broadcasted_iota(jnp.int32, (PADB, 128), 1)
    picked = jnp.where(hot, lax.broadcasted_iota(jnp.int32, (PADB, 128), 0), 0)
    chosen_v[...] = jnp.broadcast_to(jnp.max(picked, axis=0, keepdims=True), (8, 128))
    load_c = pltpu.make_async_copy(chosen_v, chosen, in_sem.at[CH + 2])
    load_c.start()
    gsq[...] = jnp.zeros_like(gsq)
    psq[...] = jnp.zeros_like(psq)
    pl.semaphore_wait(barrier, NX * NC - 1 + PAIRS - 1)
    load_c.wait()

    sends = []

    def send(src, dst, ss, rs, dev):
        c = pltpu.make_async_remote_copy(
            src_ref=src, dst_ref=dst, send_sem=ss, recv_sem=rs, device_id=dev, device_id_type=MESH
        )
        c.start()
        return c

    gnext = lax.rem(g + 1, NX) * GB
    gprev = lax.rem(g + 3, NX) * GB
    gfar = lax.rem(g + 2, NX) * GB
    gown = g * GB

    def x1(k):
        loads[k].wait()
        a = send(gin.at[k, pl.ds(gfar, HALF)], xa.at[0, k], xsnd.at[0, 0, k], xrcv.at[0, 0, k], xdev(1))
        b = send(gin.at[k, pl.ds(gfar + HALF, HALF)], xa.at[1, k], xsnd.at[0, 1, k], xrcv.at[0, 1, k], xdev(3))
        sends.extend([a, b])
        return a, b

    def x2own(k):
        a = send(
            gin.at[k, pl.ds(gnext + HALF, HALF)], xb.at[0, k, pl.ds(HALF, HALF)],
            xsnd.at[1, 0, k], xrcv.at[1, 0, k], xdev(1),
        )
        b = send(
            gin.at[k, pl.ds(gprev, HALF)], xb.at[1, k, pl.ds(0, HALF)],
            xsnd.at[1, 1, k], xrcv.at[1, 1, k], xdev(3),
        )
        sends.extend([a, b])
        return a, b

    def x2sum(k, first):
        out_c = []
        for side, base in ((0, gnext), (1, gprev + HALF)):
            first[side].wait_recv()

            @pl.loop(0, HALF, unroll=3)
            def _(i):
                xs[side, k, i] = (gin[k, base + i].astype(f32) + xa[side, k, i].astype(f32)).astype(bf16)

            at = pl.ds(0, HALF) if side == 0 else pl.ds(HALF, HALF)
            out_c.append(
                send(
                    xs.at[side, k], xb.at[side, k, at],
                    xsnd.at[2, side, k], xrcv.at[2, side, k], xdev(1 if side == 0 else 3),
                )
            )
        sends.extend(out_c)
        return out_c

    def spread(src, dst, ss, rs):
        @pl.loop(0, PAIRS - 1)
        def _(i):
            n = lax.div(i, NY)
            dz = NZ // 2 + (1 - 2 * lax.rem(n, 2)) * lax.div(n + 1, 2)
            to = pair_at(dz * NY + NY - 1 - lax.rem(i, NY))
            send(src.at[to], dst.at[pair], ss, rs, {"fsdp": to * NC + core})

    def pack_and_z(k, got):
        for c in got:
            c.wait_recv()

        @pl.loop(0, GB, unroll=4)
        def _(b):
            v = gin[k, gown + b].astype(f32) + xb[0, k, b].astype(f32) + xb[1, k, b].astype(f32)
            summed[k][b] = v.astype(bf16)

        @pl.loop(0, PAIRS, unroll=4)
        def _(p):
            for c in range(NC):
                zsend[k, p, c] = summed[k][chosen[0, p * NC + c]]

        spread(zsend.at[k], zrcv.at[k], zsnd.at[k], zrs.at[k])
        zrcv[k, pair] = zsend[k, pair]

    def wait_all(buf, sem):
        part = buf.at[pl.ds(0, PAIRS - 1)]
        pltpu.make_async_copy(part, part, sem).wait()

    swaps = {}

    def z_to_y(k):
        wait_all(zrcv.at[k], zrs.at[k])
        swaps[k] = send(zrcv.at[k, :, other], gbuf.at[k, :, core], ysnd.at[k], yrs.at[k], swap)
        gbuf[k, :, core] = zrcv[k, :, core]

    def mul_right(k):
        swaps[k].wait()
        if k == 0:
            load_f.wait()

        @pl.loop(0, 4)
        def _(i):
            part = gbuf[k, pl.ds(i * 8, 8)].reshape(256, W)
            wide = part.astype(f32)
            gsq[...] += jnp.sum((wide * wide).reshape(32, 8, W), axis=0)
            prod = jnp.dot(part, fac[1, pl.ds(k * W, W), :], preferred_element_type=f32)
            rows = pl.ds(pl.multiple_of(i * 256, 256), 256)
            if k > 0:
                prod = prod + acc[rows, :]
            if k == CH - 1:
                rp[rows, :] = prod.astype(bf16)
            else:
                acc[rows, :] = prod

    x1s, x2s = {}, {}
    x1s[0] = x1(0)
    x2s[0] = list(x2own(0))
    x1s[1] = x1(1)
    for t in range(CH + 5):
        if 0 <= t - 1 < CH:
            pack_and_z(t - 1, x2s[t - 1])
        if t < CH:
            x2s[t] += x2sum(t, x1s[t])
            if t + 1 < CH:
                x2s[t + 1] = list(x2own(t + 1))
            if t + 2 < CH:
                x1s[t + 2] = x1(t + 2)
        if 0 <= t - 4 < CH:
            z_to_y(t - 4)
        if 0 <= t - 5 < CH:
            mul_right(t - 5)

    def mul_left(j):
        @pl.loop(0, 4)
        def _(i):
            turn = lax.rem(i + lax.div(pair, 8) + 2, 4)
            rows = pl.ds(pl.multiple_of(turn * 256, 256), 256)
            prod = jnp.dot(fac[0, rows, :], rp[:, pl.ds(j * W2, W2)], preferred_element_type=f32)
            psq[...] += jnp.sum((prod * prod).reshape(32, 8, W2), axis=0)
            pbuf[j, pl.ds(turn * 8, 8)] = prod.astype(bf16).reshape(8, NC, ROWS, W2)
            if j == 0:

                @pl.loop(0, 8)
                def _(n):
                    to = turn * 8 + lax.rem(n + pair, 8)

                    @pl.when(to != pair)
                    def _():
                        send(pbuf.at[j, to], yrcv.at[j, pair], csnd.at[j], crs.at[j], {"fsdp": to * NC + core})

        if j > 0:
            spread(pbuf.at[j], yrcv.at[j], csnd.at[j], crs.at[j])
        yrcv[j, pair] = pbuf[j, pair]

    def y_to_z(j):
        wait_all(yrcv.at[j], crs.at[j])
        swaps[j] = send(yrcv.at[j, :, other], fin[j].at[:, core], dsnd.at[j], drs.at[j], swap)
        fin[j][:, core] = yrcv[j, :, core]

    def exchange(buf_a, buf_b, value, merge, row):
        me = g * NC + core
        buf_a[me] = value
        got = [
            send(buf_a.at[me], buf_a.at[me], ea_snd.at[row, d], ea_rcv.at[row, d], xcdev(d))
            for d in range(1, NX * NC)
        ]
        sends.extend(got)
        for c in got:
            c.wait_recv()
        buf_b[pair] = merge(buf_a[...])

        @pl.loop(1, PAIRS)
        def _(d):
            to = pair_at(d)
            send(buf_b.at[pair], buf_b.at[pair], eb_snd.at[row], eb_rcv.at[row], {"fsdp": to * NC + core})

        wait_all(buf_b, eb_rcv.at[row])

    for j in range(CJ):
        mul_left(j)

    lane = lax.broadcasted_iota(jnp.int32, (8, 128), 1)
    sub = lax.broadcasted_iota(jnp.int32, (8, 128), 0)
    used = jnp.sum(jnp.where(hot, 1.0, 0.0), axis=0, keepdims=True)
    gtot = jnp.sum(gsq[...], keepdims=True)
    ptot = jnp.sum(psq[...], keepdims=True)
    mine = jnp.where(sub == 0, gtot * used, jnp.where(sub == 1, ptot, 0.0))
    lead = lax.broadcasted_iota(jnp.int32, (NX * NC, 8, 128), 0)

    def merge(t):
        plane = jnp.sum(jnp.where(lax.div(lead, NC) == g, t, 0.0), axis=0)
        return jnp.where(sub == 2, jnp.sum(t, axis=0)[0:1, :], plane)

    exchange(sta, stb, jnp.where(lane == f, mine, 0.0), merge, 0)
    for j in range(CJ):
        y_to_z(j)
    plane = jnp.sum(stb[...], axis=0)
    squares = jnp.sum(plane[2:3, :], axis=1, keepdims=True)
    scale = 0.5 * math.sqrt(float(NX * GB * BS * BS)) / jnp.sqrt(squares)
    count = float(BS * BS)
    ratio = jnp.sqrt((plane[0:1, :] / count + small_eps) / (plane[1:2, :] / count + small_eps))
    per_block = jnp.sum(jnp.where(hot, scale * ratio, 0.0), axis=1, keepdims=True)
    sc[...] = jnp.broadcast_to(per_block, (PADB, W2))
    bmax[...] = jnp.zeros_like(bmax)
    load_w.wait()

    stores = []
    for j in range(CJ):
        swaps[j].wait_recv()
        cols = pl.ds(j * W2, W2)

        @pl.loop(0, GB, unroll=4)
        def _(b):
            o = owner[g * GB + b]
            u = fin[j][lax.div(o, NC), lax.rem(o, NC)].astype(f32)
            upd = (sc[pl.ds(b, 1), :] * u).astype(bf16).astype(f32)
            nw = (win[b, :, cols].astype(f32) - learn_rate * upd).astype(bf16)
            fresh[b, :, cols] = nw
            mag = jnp.abs(nw.astype(f32))
            mag = jnp.maximum(mag[0:8], mag[8:16])
            m = bmax[b]
            for s in range(W2 // 128):
                m = jnp.maximum(m, mag[:, s * 128 : (s + 1) * 128])
            bmax[b] = m

        stores.append(pltpu.make_async_copy(fresh.at[:, :, cols], out.at[:, :, cols], in_sem.at[CH + 3 + j]))
        stores[j].start()

    bid = lax.broadcasted_iota(jnp.int32, (GB, 8, 128), 0) + g * GB
    peak = bmax[...]
    tile = jnp.zeros((8, 128), f32)
    edges = (0, 64, 72, 80, 144)
    for t in range(4):
        inside = (bid >= edges[t]) & (bid < edges[t + 1])
        m = jnp.max(jnp.max(jnp.where(inside, peak, 0.0), axis=0), axis=0, keepdims=True)
        tile = jnp.where(sub == t, m, tile)
    exchange(mxa, mxb, tile, lambda t: jnp.max(t, axis=0), 1)
    scale = 1.0 / (jnp.max(jnp.max(mxb[...], axis=0), axis=1, keepdims=True) + small_eps)
    rid = lax.broadcasted_iota(jnp.int32, (PADB, 128), 0) + g * GB
    inv = jnp.zeros((PADB, 128), f32)
    for t in range(4):
        inside = (rid >= edges[t]) & (rid < edges[t + 1])
        inv = jnp.where(inside, scale[t : t + 1, :], inv)
    inv_out[...] = inv
    for c in stores:
        c.wait()

    for c in sends:
        c.wait_send()
    for k in range(CH):
        wait_all(zsend.at[k], zsnd.at[k])
    for k in range(CJ):
        wait_all(pbuf.at[k], csnd.at[k])
        swaps[k].wait_send()
    for row, buf in ((0, stb), (1, mxb)):
        wait_all(buf, eb_snd.at[row])


def rescale(weight, inv, out):
    @pl.loop(0, GB, unroll=4)
    def _(b):
        s = inv[pl.ds(b, 1), :]
        for c in range(BS // 128):
            at = pl.ds(c * 128, 128)
            out[b, :, at] = (weight[b, :, at].astype(f32) * s).astype(bf16)


def per_device(grad_parts, factors, weights, block_owner):
    smem = pl.BlockSpec(memory_space=pltpu.SMEM)
    vmem = pl.BlockSpec(memory_space=pltpu.VMEM)
    hbm = pl.BlockSpec(memory_space=pl.ANY)
    dma = pltpu.SemaphoreType.DMA
    new_weight, inv = pl.pallas_call(
        kernel,
        out_shape=(jax.ShapeDtypeStruct((GB, ROWS, BS), bf16), jax.ShapeDtypeStruct((PADB, 128), f32)),
        in_specs=[smem, hbm, hbm, hbm],
        out_specs=(hbm, vmem),
        scratch_shapes=[
            pltpu.VMEM((CH, NX * GB, ROWS, W), bf16),
            pltpu.VMEM((2, BS, BS), bf16),
            pltpu.VMEM((GB, ROWS, BS), bf16),
            pltpu.VMEM((2, CH, HALF, ROWS, W), bf16),
            pltpu.VMEM((2, CH, HALF, ROWS, W), bf16),
            pltpu.VMEM((2, CH, GB, ROWS, W), bf16),
            [pltpu.VMEM((GB, ROWS, W), bf16)] * CH,
            pltpu.VMEM((CH, PAIRS, NC, ROWS, W), bf16),
            pltpu.VMEM((CH, PAIRS, NC, ROWS, W), bf16),
            pltpu.VMEM((CH, PAIRS, NC, ROWS, W), bf16),
            pltpu.VMEM((BS, BS), f32),
            pltpu.VMEM((BS, BS), bf16),
            pltpu.VMEM((CJ, PAIRS, NC, ROWS, W2), bf16),
            pltpu.VMEM((CJ, PAIRS, NC, ROWS, W2), bf16),
            [pltpu.VMEM((PAIRS, NC, ROWS, W2), bf16)] * CJ,
            pltpu.VMEM((8, W), f32),
            pltpu.VMEM((8, W2), f32),
            pltpu.VMEM((PADB, W2), f32),
            pltpu.VMEM((GB, 8, 128), f32),
            pltpu.VMEM((NX * NC, 8, 128), f32),
            pltpu.VMEM((PAIRS, 8, 128), f32),
            pltpu.VMEM((NX * NC, 8, 128), f32),
            pltpu.VMEM((PAIRS, 8, 128), f32),
            pltpu.VMEM((PADB, 128), jnp.int32),
            pltpu.VMEM((8, 128), jnp.int32),
            pltpu.SMEM((8, 128), jnp.int32),
            pltpu.VMEM((GB, ROWS, BS), bf16),
            dma((CH + 3 + CJ,)),
            dma((3, 2, CH)),
            dma((3, 2, CH)),
            dma((CH,)),
            dma((CH,)),
            dma((CH,)),
            dma((CH,)),
            dma((CH,)),
            dma((CH,)),
            dma((CH,)),
            dma((CH,)),
            dma((2, 8)),
            dma((2, 8)),
            dma((2,)),
            dma((2,)),
        ],
        compiler_params=pltpu.CompilerParams(
            collective_id=0, has_side_effects=True, vmem_limit_bytes=56 * 2**20
        ),
        cost_estimate=pl.CostEstimate(flops=4 * BS**3, bytes_accessed=12 * 2**20, transcendentals=0),
        name="shampoo_step",
    )(block_owner, grad_parts[0], factors.reshape(2, BS, BS), weights)
    return pl.pallas_call(
        rescale,
        out_shape=jax.ShapeDtypeStruct((GB, ROWS, BS), bf16),
        in_specs=[vmem, vmem],
        out_specs=vmem,
        cost_estimate=pl.CostEstimate(flops=GB * ROWS * BS, bytes_accessed=3 * 2**20, transcendentals=0),
        name="rescale",
    )(new_weight, inv)


def solution(mesh):
    placed = (
        P("dp", None, "fsdp", None),
        P("dp", "fsdp", None, None, None, None),
        P("dp", "fsdp", None),
        P(),
    )
    return jax.shard_map(
        per_device, mesh=mesh, in_specs=placed, out_specs=P("dp", "fsdp", None), check_vma=False
    )
```
